32 devices in a mesh: groups: 2 (over y), section: 4 (over z), replica: 2 (over x), tensor: 2 (over core).
Axes of the slice: x: 2, y: 2, z: 4, core: 2. Of those that a mesh axis runs over, the one named last changes fastest.
Arguments:
- inflow: bfloat16 [4, 1024, 1152], P('section', ('groups', 'replica')), parts along dimension 1, may hold values from -6 to 6
- fresh_rows: bfloat16 [2, 4, 256, 1152], P(None, ('groups', 'replica'), 'section'), parts along dimension 1, may hold values from -6 to 6
- lin_weight: bfloat16 [4, 1152, 1152], P('section', None, 'tensor'), may hold values from -0.125 to 0.125
- qkv_weight: bfloat16 [4, 3, 1152, 576], P('section', None, None, 'tensor'), may hold values from -2 to 2
- out_weight: bfloat16 [4, 576, 1152], P('section', 'tensor'), may hold values from -0.25 to 0.25
- mod_weight: bfloat16 [4, 128, 2, 1152], P('section', None, None, 'tensor'), may hold values from -0.5 to 0.5
- plan: int32 [3, 4], P(None, 'section'), may hold values from 0 to 5
- timesteps: int32 [6, 4], P(None, ('groups', 'replica')), parts along dimension 1, may hold values from 0 to 999
Outputs:
- settled: float32 [4, 1024, 1152], P('section', ('groups', 'replica'), 'tensor'), parts along dimension 1
The draws below stay inside these ranges and needn't reach their ends.
There are 2 independent parts, one for each index of `groups`. The reference program is written for one: setup_inputs(seed, part) draws one part's arguments, and reference() takes and returns one part's arrays. A program takes and returns all parts, laid end to end along the dimension named above; an argument that names none is the same for every part. Nothing has to cross between parts.
All inputs are finite; a program needn't handle non-finite values.
Results may differ from the reference program's by a relative error of at most 0.039.
Values may be sent and summed in bfloat16 or wider, within the bound.
A program may use at most 64 MiB of HBM per device.

```python
import math
import jax
import jax.numpy as jnp
from jax import lax

D = 1152
DH = 72
HEADS = 8
HD = 576
FREQ = 128
NT = 1000
TOKS = 256
TICKS = 3
IMAGES = 2
ROWS = 512
SECTIONS = 4
MICRO = 6
N_TENSOR = 2


def draw_qkv_weight(key, part):
    key_list = jax.random.split(key, 1)
    shaped = jax.random.normal(key_list[0], (SECTIONS, 3, D, HD), jnp.float32) * (1.0 / math.sqrt(D))
    return jnp.clip(shaped, -2.0, 2.0).astype(jnp.bfloat16)


def touch_ends(entries, rng, smallest, largest):
    longest = entries.shape.index(max(entries.shape))
    spots = []
    for shift in (0, 1):
        where = [jax.random.randint(jax.random.fold_in(rng, axis), (), 0, length) for axis, length in enumerate(entries.shape)]
        where[longest] = (where[longest] + shift) % entries.shape[longest]
        spots.append(tuple(where))
    return entries.at[spots[0]].set(smallest).at[spots[1]].set(largest)


def level_of(own_key, extent, cuts, least, high):
    def one(dim, parts):
        steps = jax.random.uniform(jax.random.fold_in(jax.random.fold_in(own_key, 6), dim), (parts,), jnp.float32, least / len(cuts), high / len(cuts))
        return jnp.repeat(jnp.exp(steps), extent[dim] // parts).reshape((-1,) + (1,) * (len(extent) - dim - 1))

    factor_of = one(*cuts[0])
    for cut in cuts[1:]:
        factor_of = factor_of * one(*cut)
    return factor_of


def normal_values(key, shape, deviation, reach, cuts=(), held_as=jnp.bfloat16):
    values = deviation * jax.random.normal(key, shape, jnp.float32)
    if cuts:
        values = values * level_of(key, shape, cuts, -0.22, 0.18)
    return jnp.clip(values, -reach, reach).astype(held_as)


def setup_inputs(seed: int = 0, part: int = 0) -> dict:
    arg_keys = jax.random.split(jax.random.key(seed), 9)
    part_keys = jax.random.split(jax.random.fold_in(arg_keys[8], part), 9)
    return {
        "inflow": normal_values(part_keys[0], (SECTIONS, ROWS, D), 1.0, 6.0, ((0, 4), (1, 2))),
        "fresh_rows": normal_values(part_keys[1], (TICKS - 1, IMAGES, TOKS, D), 1.0, 6.0, ((1, 2), (2, 4))),
        "lin_weight": normal_values(arg_keys[2], (SECTIONS, D, D), (2 * D) ** -0.5, 0.125, ((0, 4), (2, 2))),
        "qkv_weight": draw_qkv_weight(jax.random.fold_in(arg_keys[8], 71), part),
        "out_weight": normal_values(arg_keys[4], (SECTIONS, HD, D), HD ** -0.5, 0.25, ((0, 4), (1, 2))),
        "mod_weight": normal_values(arg_keys[5], (SECTIONS, FREQ, 2, D), FREQ ** -0.5, 0.5, ((0, 4), (3, 2))),
        "plan": touch_ends(jax.random.randint(arg_keys[6], (TICKS, SECTIONS), 0, MICRO), jax.random.fold_in(arg_keys[6], 1), 0, MICRO - 1).astype(jnp.int32),
        "timesteps": touch_ends(jax.random.randint(part_keys[7], (MICRO, IMAGES), 0, NT), jax.random.fold_in(part_keys[7], 1), 0, NT - 1).astype(jnp.int32),
    }


epsilon = 1e-06

def timestep_embed(times):
    half_width = FREQ // 2
    frequency = jnp.exp(-math.log(10000.0) * jnp.arange(half_width, dtype=jnp.float32) / half_width)
    phases = times.astype(jnp.float32)[:, None] * frequency[None, :]
    return jnp.concatenate([jnp.cos(phases), jnp.sin(phases)], axis=1)

def attention_block(arrays):
    hidden, modulation, weights_qkv, weights_out = arrays
    image_count = modulation.shape[0]
    widths = hidden.shape[1]
    values_f = hidden.reshape(image_count, TOKS, widths)
    centred = values_f - lax.optimization_barrier(jnp.mean(values_f, axis=-1, keepdims=True))
    variance = lax.optimization_barrier(jnp.mean(centred * centred, axis=-1, keepdims=True))
    normed = centred * lax.rsqrt(variance + epsilon)
    scaling = modulation[:, 0].astype(jnp.float32)[:, None, :]
    gating = modulation[:, 1].astype(jnp.float32)[:, None, :]
    mixed = (normed * (1.0 + scaling)).astype(jnp.bfloat16).reshape(-1, widths)
    projected = [jnp.dot(mixed, weights_qkv[index], preferred_element_type=jnp.float32).astype(jnp.bfloat16).reshape(image_count, TOKS, HEADS, DH) for index in range(3)]
    scores = jnp.einsum('iqhe,ikhe->ihqk', projected[0].astype(jnp.float32), projected[1].astype(jnp.float32)) * (1.0 / math.sqrt(DH))
    weights_soft = jax.nn.softmax(scores, axis=-1).astype(jnp.bfloat16)
    attended = jnp.einsum('ihqk,ikhe->iqhe', weights_soft.astype(jnp.float32), projected[2].astype(jnp.float32)).astype(jnp.bfloat16).reshape(-1, HEADS * DH)
    group_cols = HEADS * DH // N_TENSOR
    summed = jnp.zeros((attended.shape[0], widths), jnp.float32)
    for group in range(N_TENSOR):
        lower = group * group_cols
        piece = jnp.dot(attended[:, lower:lower + group_cols], weights_out[lower:lower + group_cols], preferred_element_type=jnp.float32)
        summed = summed + lax.optimization_barrier(piece.astype(jnp.bfloat16)).astype(jnp.float32)
    result = values_f + gating * summed.reshape(image_count, TOKS, widths)
    return result.reshape(-1, widths)

def section_product(couple):
    return jnp.dot(couple[0].astype(jnp.bfloat16), couple[1], preferred_element_type=jnp.float32)

def reference(inflow, fresh_rows, lin_weight, qkv_weight, out_weight, mod_weight, plan, timesteps):
    section_count = inflow.shape[0]
    upper = (jnp.arange(section_count) >= section_count // 2)[:, None, None]
    current = inflow.astype(jnp.float32)
    settled = current
    for tick_index in range(TICKS):
        products = lax.map(section_product, (current, lin_weight))
        skipped = products[::-1]
        hidden = jnp.where(upper, products + skipped, current)
        times = timesteps[plan[tick_index]]
        embedded = timestep_embed(times.reshape(-1)).reshape(section_count, -1, FREQ)
        modulation = jnp.einsum('sif,sfcd->sicd', embedded, mod_weight.astype(jnp.float32), precision=lax.Precision.HIGHEST).astype(jnp.bfloat16)
        settled = lax.map(attention_block, (hidden, modulation, qkv_weight, out_weight))
        if tick_index + 1 < TICKS:
            arriving = fresh_rows[tick_index].astype(jnp.float32).reshape(1, -1, settled.shape[2])
            current = jnp.concatenate([arriving, settled[:-1]], axis=0)
    return settled
```

```python
import functools
import math

import jax
import jax.numpy as jnp
from jax import lax
from jax.experimental import pallas as pl
from jax.experimental.pallas import tpu as pltpu
from jax.sharding import PartitionSpec as P

DH = 72
FREQ = 128
TICKS = 3
epsilon = 1e-06
F32 = jnp.float32
BF16 = jnp.bfloat16


def timestep_embed(times):
    half_width = FREQ // 2
    frequency = jnp.exp(-math.log(10000.0) * jnp.arange(half_width, dtype=F32) / half_width)
    phases = times.astype(F32)[:, None] * frequency[None, :]
    return jnp.concatenate([jnp.cos(phases), jnp.sin(phases)], axis=1)


def dot(a, b):
    return jnp.dot(a, b, preferred_element_type=F32)


def kernel(
    sections,
    inflow_ref,
    fresh_ref,
    lin_ref,
    qkv_ref,
    out_w_ref,
    mod_ref,
    out_ref,
    lin_other,
    lin_full,
    out_split,
    mod_other,
    mod_full,
    fresh_in,
    xin,
    skip_out,
    skip_in,
    hidden,
    u_buf,
    q_buf,
    k_buf,
    v_buf,
    g_out,
    g_in,
    gl_out,
    gl_in,
    h_cols,
    h_in,
    y_out,
    lin_sem,
    mod_sem,
    fresh_send,
    fresh_recv,
    x_send,
    x_recv,
    skip_send,
    skip_recv,
    u_send,
    u_recv,
    g_send,
    g_recv,
    gl_send,
    gl_recv,
    h_sem,
):
    s = lax.axis_index("section")
    c = lax.axis_index("tensor")
    o = 1 - c
    half = sections // 2
    mirror = sections - 1 - s
    down = s < half
    rows = inflow_ref.shape[1]
    width = inflow_ref.shape[2]
    half_width = width // 2
    heads = out_w_ref.shape[0] // DH
    head_cols = out_w_ref.shape[0]
    last = TICKS - 1

    def remote(src, dst, send, recv, device):
        return pltpu.make_async_remote_copy(
            src_ref=src,
            dst_ref=dst,
            send_sem=send,
            recv_sem=recv,
            device_id=device,
            device_id_type=pl.DeviceIdType.MESH,
        )

    fresh_sender = (s > 0) & (s // half == c)

    barrier = pltpu.get_barrier_semaphore()

    def greet(device):
        pl.semaphore_signal(
            barrier, inc=1, device_id=device, device_id_type=pl.DeviceIdType.MESH
        )

    greet({"tensor": o})
    greet({"section": mirror})

    @pl.when(s > 0)
    def _():
        greet({"section": s - 1})

    @pl.when(s < sections - 1)
    def _():
        greet({"section": s + 1})

    @pl.when(fresh_sender)
    def _():
        greet({"section": 0})

    @pl.when(s == 0)
    def _():
        for block in range(half):

            @pl.when((c * half + block) > 0)
            def _():
                greet({"section": c * half + block})

    expected = (
        2
        + jnp.where(s > 0, 1, 0)
        + jnp.where(s < sections - 1, 1, 0)
        + jnp.where(fresh_sender, 1, 0)
        + jnp.where(s == 0, half - 1 + c, 0)
    )
    pl.semaphore_wait(barrier, expected)

    def fresh_copy(tick, block):
        return remote(
            fresh_ref.at[tick],
            fresh_in.at[tick, block],
            fresh_send.at[tick],
            fresh_recv.at[tick, block],
            {"section": 0},
        )

    @pl.when(fresh_sender)
    def _():
        for tick in range(TICKS - 1):
            fresh_copy(tick, s % half).start()

    lin_copy = remote(lin_ref, lin_other, lin_sem.at[0], lin_sem.at[1], {"tensor": o})
    mod_copy = remote(mod_ref, mod_other, mod_sem.at[0], mod_sem.at[1], {"tensor": o})
    mod_copy.start()

    out_split[0] = out_w_ref[:, :half_width]
    out_split[1] = out_w_ref[:, half_width:]
    xin[0] = inflow_ref[c]
    mod_copy.wait()

    @pl.when(c == 0)
    def _():
        mod_full[...] = jnp.concatenate([mod_ref[...], mod_other[...]], axis=1)

    @pl.when(c == 1)
    def _():
        mod_full[...] = jnp.concatenate([mod_other[...], mod_ref[...]], axis=1)

    def skip_copy(tick):
        return remote(
            skip_out.at[tick],
            skip_in.at[tick],
            skip_send.at[tick],
            skip_recv.at[tick],
            {"section": mirror},
        )

    def x_copy(tick):
        return remote(
            y_out.at[tick],
            xin.at[tick + 1],
            x_send.at[tick],
            x_recv.at[tick],
            {"section": s + 1},
        )

    def x_wait(tick):
        remote(
            y_out.at[tick],
            xin.at[tick + 1],
            x_send.at[tick],
            x_recv.at[tick],
            {"section": s - 1},
        ).wait_recv()

    def linear(tick):
        return dot(xin[tick], lin_full[...])

    def fresh_arrive(tick):
        for block in range(half):

            @pl.when((c * half + block) > 0)
            def _():
                remote(
                    fresh_ref.at[tick],
                    fresh_in.at[tick, block],
                    fresh_send.at[tick],
                    fresh_recv.at[tick, block],
                    {"section": c * half + block},
                ).wait_recv()

        @pl.when(c == 0)
        def _():
            fresh_in[tick, 0] = fresh_ref[tick]

        xin[tick + 1] = fresh_in[tick].astype(F32).reshape(rows, width).astype(BF16)

    lane_head = lax.broadcasted_iota(jnp.int32, (rows, head_cols), 1)
    head_masks = [(lane_head >= DH * h) & (lane_head < DH * (h + 1)) for h in range(heads)]
    scale = 1.0 / math.sqrt(DH)

    def attend(part):
        q = q_buf[part]
        k = k_buf[...].reshape(2 * rows, head_cols)
        v = v_buf[...].reshape(2 * rows, head_cols)
        total = None
        for h in range(heads):
            q_h = jnp.where(head_masks[h], q, jnp.zeros_like(q))
            scores = (
                lax.dot_general(q_h, k, (((1,), (1,)), ((), ())), preferred_element_type=F32)
                * scale
            )
            top = jnp.max(scores, axis=-1, keepdims=True)
            grown = jnp.exp(scores - top)
            soft = (grown / jnp.sum(grown, axis=-1, keepdims=True)).astype(BF16)
            product = dot(soft, v)
            total = product if h == 0 else jnp.where(head_masks[h], product, total)
        return total.astype(BF16)

    def u_copy(tick):
        return remote(
            u_buf.at[tick, c], u_buf.at[tick, c], u_send.at[tick], u_recv.at[tick], {"tensor": o}
        )

    def u_wait(tick):
        remote(
            u_buf.at[tick, o], u_buf.at[tick, o], u_send.at[tick], u_recv.at[tick], {"tensor": o}
        ).wait_recv()

    def project(tick, part):
        rows_in = u_buf[tick, part]
        q_buf[part] = dot(rows_in, qkv_ref[0]).astype(BF16)
        k_buf[part] = dot(rows_in, qkv_ref[1]).astype(BF16)
        v_buf[part] = dot(rows_in, qkv_ref[2]).astype(BF16)

    def h_copy():
        return remote(h_cols.at[o], h_in, h_sem.at[0], h_sem.at[1], {"tensor": o})

    def block(tick):
        values = hidden[...]
        centred = values - jnp.mean(values, axis=-1, keepdims=True)
        variance = jnp.mean(centred * centred, axis=-1, keepdims=True)
        normed = centred * lax.rsqrt(variance + epsilon)
        scaling = mod_full[2 * tick : 2 * tick + 1, :]
        u_buf[tick, c] = (normed * (1.0 + scaling)).astype(BF16)
        u_copy(tick).start()
        project(tick, c)
        if tick == last:
            h_cols[0] = hidden[:, :half_width]
            h_cols[1] = hidden[:, half_width:]
            h_copy().start()
        u_wait(tick)
        project(tick, o)

    def g_copy(tick):
        return remote(
            g_out.at[tick], g_in.at[tick], g_send.at[tick], g_recv.at[tick], {"tensor": o}
        )

    def relay(tick):
        g_out[tick] = dot(attend(o), out_w_ref[...]).astype(BF16)
        g_copy(tick).start()
        own = dot(attend(c), out_w_ref[...]).astype(BF16).astype(F32)
        gating = mod_full[2 * tick + 1 : 2 * tick + 2, :]
        g_copy(tick).wait_recv()
        y = hidden[...] + gating * (own + g_in[tick].astype(F32))
        y_out[tick] = y.astype(BF16)
        x_copy(tick).start()

    def gl_copy(part):
        return remote(
            gl_out.at[part], gl_in.at[part], gl_send.at[part], gl_recv.at[part], {"tensor": o}
        )

    def settle():
        gating = mod_ref[2 * last + 1 : 2 * last + 2, :]
        for part in range(2):
            heads_out = attend(part)
            gl_out[part] = dot(heads_out, out_split[o]).astype(BF16)
            gl_copy(part).start()
            out_ref[part] = dot(heads_out, out_split[c]).astype(BF16).astype(F32)
        h_copy().wait_recv()
        for part in range(2):
            gl_copy(part).wait_recv()
            summed = out_ref[part] + gl_in[part].astype(F32)
            h_part = jnp.where(c == part, h_cols[c], h_in[...])
            out_ref[part] = h_part + gating * summed

    def skip_needed(tick):
        return down & (mirror <= sections - TICKS + tick)

    def send_skip(tick):
        skip_out[tick] = linear(tick).astype(BF16)
        skip_copy(tick).start()

    lin_copy.start()

    for tick in range(TICKS):
        live = s <= sections - TICKS + tick

        @pl.when((s > 0) & live)
        def _():
            if tick > 0:
                x_wait(tick - 1)

        def prepare_linear():
            lin_copy.wait()

            @pl.when(c == 0)
            def _():
                lin_full[...] = jnp.concatenate([lin_ref[...], lin_other[...]], axis=1)

            @pl.when(c == 1)
            def _():
                lin_full[...] = jnp.concatenate([lin_other[...], lin_ref[...]], axis=1)

        if tick == 0:
            first_linear = skip_needed(0) | (jnp.logical_not(down))

            @pl.when(first_linear)
            def _():
                prepare_linear()

        if tick > 0:

            @pl.when(skip_needed(tick) & (s > 0))
            def _():
                send_skip(tick)

        else:

            @pl.when(skip_needed(tick))
            def _():
                send_skip(tick)

        @pl.when(live & down)
        def _():
            hidden[...] = xin[tick].astype(F32)

        @pl.when(live & jnp.logical_not(down))
        def _():
            own = linear(tick)
            remote(
                skip_out.at[tick],
                skip_in.at[tick],
                skip_send.at[tick],
                skip_recv.at[tick],
                {"section": mirror},
            ).wait_recv()
            hidden[...] = own + skip_in[tick].astype(F32)

        if tick < last:

            @pl.when(live)
            def _():
                block(tick)
                relay(tick)

        else:
            block(tick)
            settle()

        if tick == 0:

            @pl.when(jnp.logical_not(first_linear))
            def _():
                prepare_linear()

            @pl.when(s == 0)
            def _():
                for later in range(TICKS - 1):
                    fresh_arrive(later)
                for later in range(1, TICKS):

                    @pl.when(skip_needed(later))
                    def _():
                        send_skip(later)

    @pl.when(fresh_sender)
    def _():
        for tick in range(TICKS - 1):
            fresh_copy(tick, s % half).wait_send()

    h_copy().wait_send()
    for part in range(2):
        gl_copy(part).wait_send()
    for tick in range(TICKS):

        @pl.when(skip_needed(tick))
        def _():
            skip_copy(tick).wait_send()

        @pl.when(s <= sections - TICKS + tick)
        def _():
            u_copy(tick).wait_send()
            if tick < last:
                g_copy(tick).wait_send()
                x_copy(tick).wait_send()


def on_device(inflow, fresh_rows, lin_weight, qkv_weight, out_weight, mod_weight, plan, timesteps):
    sections = lax.axis_size("section")
    row_count, width = inflow.shape[1:]
    rows = row_count // 2
    half_width = lin_weight.shape[2]
    head_cols = out_weight.shape[1]
    half = sections // 2
    piece = fresh_rows.shape[2]
    micro_ids = lax.broadcasted_iota(jnp.int32, (TICKS, timesteps.shape[0]), 1)
    times = jnp.sum(jnp.where(micro_ids == plan, timesteps[:, 0][None, :], 0), axis=1)
    modulation = (
        jnp.einsum(
            "tf,fcd->tcd",
            timestep_embed(times),
            mod_weight[0].astype(F32),
            precision=lax.Precision.HIGHEST,
        )
        .astype(BF16)
        .astype(F32)
        .reshape(2 * TICKS, half_width)
    )
    modulation = jnp.pad(modulation, ((0, 8 - 2 * TICKS), (0, 0)))
    vmem = pl.BlockSpec(memory_space=pltpu.VMEM)
    dma = pltpu.SemaphoreType.DMA
    settled = pl.pallas_call(
        functools.partial(kernel, sections),
        out_shape=jax.ShapeDtypeStruct((2, rows, half_width), F32),
        in_specs=[vmem] * 6,
        out_specs=vmem,
        scratch_shapes=[
            pltpu.VMEM((width, half_width), BF16),
            pltpu.VMEM((width, width), BF16),
            pltpu.VMEM((2, head_cols, half_width), BF16),
            pltpu.VMEM((8, half_width), F32),
            pltpu.VMEM((8, width), F32),
            pltpu.VMEM((TICKS - 1, half, piece, width), BF16),
            pltpu.VMEM((TICKS, rows, width), BF16),
            pltpu.VMEM((TICKS, rows, width), BF16),
            pltpu.VMEM((TICKS, rows, width), BF16),
            pltpu.VMEM((rows, width), F32),
            pltpu.VMEM((TICKS, 2, rows, width), BF16),
            pltpu.VMEM((2, rows, head_cols), BF16),
            pltpu.VMEM((2, rows, head_cols), BF16),
            pltpu.VMEM((2, rows, head_cols), BF16),
            pltpu.VMEM((TICKS - 1, rows, width), BF16),
            pltpu.VMEM((TICKS - 1, rows, width), BF16),
            pltpu.VMEM((2, rows, half_width), BF16),
            pltpu.VMEM((2, rows, half_width), BF16),
            pltpu.VMEM((2, rows, half_width), F32),
            pltpu.VMEM((rows, half_width), F32),
            pltpu.VMEM((TICKS - 1, rows, width), BF16),
            dma((2,)),
            dma((2,)),
            dma((TICKS - 1,)),
            dma((TICKS - 1, half)),
            dma((TICKS - 1,)),
            dma((TICKS - 1,)),
            dma((TICKS,)),
            dma((TICKS,)),
            dma((TICKS,)),
            dma((TICKS,)),
            dma((TICKS - 1,)),
            dma((TICKS - 1,)),
            dma((2,)),
            dma((2,)),
            dma((2,)),
        ],
        compiler_params=pltpu.CompilerParams(
            collective_id=0, has_side_effects=True, vmem_limit_bytes=44 * 2**20
        ),
    )(
        inflow[0].reshape(2, rows, width),
        fresh_rows[:, 0],
        lin_weight[0],
        qkv_weight[0],
        out_weight[0],
        modulation,
    )
    return settled.reshape(1, row_count, half_width)


def solution(mesh):
    return jax.shard_map(
        on_device,
        mesh=mesh,
        in_specs=(
            P("section", ("groups", "replica"), None),
            P(None, ("groups", "replica"), "section", None),
            P("section", None, "tensor"),
            P("section", None, None, "tensor"),
            P("section", "tensor", None),
            P("section", None, None, "tensor"),
            P(None, "section"),
            P(None, ("groups", "replica")),
        ),
        out_specs=P("section", ("groups", "replica"), "tensor"),
        check_vma=False,
    )
```

```python
import functools
import math

import jax
import jax.numpy as jnp
from jax import lax
from jax.experimental import pallas as pl
from jax.experimental.pallas import tpu as pltpu
from jax.sharding import PartitionSpec as P

DH = 72
FREQ = 128
TICKS = 3
epsilon = 1e-06
F32 = jnp.float32
BF16 = jnp.bfloat16


def dot(a, b):
    return jnp.dot(a, b, preferred_element_type=F32)


def dot_t(a, b):
    return lax.dot_general(a, b, (((1,), (1,)), ((), ())), preferred_element_type=F32)


def kernel(
    sections,
    inflow_hbm,
    fresh_ref,
    lin_ref,
    qkv_hbm,
    out_w_hbm,
    mod_hbm,
    plan_ref,
    times_ref,
    out_ref,
    qkv_ref,
    out_w_ref,
    mod_w,
    load_sem,
    lin_full,
    out_split,
    mod_buf,
    mod_full,
    gate_cols,
    fresh_in,
    xin,
    skip_out,
    skip_in,
    hidden,
    u_buf,
    q_buf,
    k_buf,
    v_buf,
    g_out,
    g_in,
    gl_out,
    gl_in,
    h_cols,
    h_in,
    y_out,
    lin_sem,
    mod_sem,
    fresh_send,
    fresh_recv,
    x_send,
    x_recv,
    skip_send,
    skip_recv,
    u_send,
    u_recv,
    g_send,
    g_recv,
    gl_send,
    gl_recv,
    h_sem,
):
    s = lax.axis_index("section")
    c = lax.axis_index("tensor")
    o = 1 - c
    half = sections // 2
    mirror = sections - 1 - s
    down = s < half
    rows = inflow_hbm.shape[1]
    width = inflow_hbm.shape[2]
    half_width = width // 2
    heads = out_w_ref.shape[0] // DH
    head_cols = out_w_ref.shape[0]
    last = TICKS - 1

    loads = [
        pltpu.make_async_copy(inflow_hbm.at[c], xin.at[0], load_sem.at[0]),
        pltpu.make_async_copy(mod_hbm, mod_w, load_sem.at[1]),
        pltpu.make_async_copy(qkv_hbm, qkv_ref, load_sem.at[2]),
        pltpu.make_async_copy(out_w_hbm, out_w_ref, load_sem.at[3]),
        pltpu.make_async_copy(lin_ref, lin_full.at[c], load_sem.at[4]),
    ]
    for load in loads:
        load.start()

    def remote(src, dst, send, recv, device):
        return pltpu.make_async_remote_copy(
            src_ref=src,
            dst_ref=dst,
            send_sem=send,
            recv_sem=recv,
            device_id=device,
            device_id_type=pl.DeviceIdType.MESH,
        )

    fresh_sender = (s > 0) & (s // half == c)

    barrier = pltpu.get_barrier_semaphore()

    def greet(device):
        pl.semaphore_signal(
            barrier, inc=1, device_id=device, device_id_type=pl.DeviceIdType.MESH
        )

    greet({"tensor": o})
    greet({"section": mirror})

    @pl.when(s > 0)
    def _():
        greet({"section": s - 1})

    @pl.when(s < sections - 1)
    def _():
        greet({"section": s + 1})

    @pl.when(fresh_sender)
    def _():
        greet({"section": 0})

    @pl.when(s == 0)
    def _():
        for block in range(half):

            @pl.when((c * half + block) > 0)
            def _():
                greet({"section": c * half + block})

    expected = (
        2
        + jnp.where(s > 0, 1, 0)
        + jnp.where(s < sections - 1, 1, 0)
        + jnp.where(fresh_sender, 1, 0)
        + jnp.where(s == 0, half - 1 + c, 0)
    )
    pl.semaphore_wait(barrier, expected)

    def fresh_copy(tick, block):
        return remote(
            fresh_ref.at[tick],
            fresh_in.at[tick, block],
            fresh_send.at[tick],
            fresh_recv.at[tick, block],
            {"section": 0},
        )

    @pl.when(fresh_sender)
    def _():
        for tick in reversed(range(TICKS - 1)):
            fresh_copy(tick, s % half).start()

    lin_copy = remote(lin_ref, lin_full.at[c], lin_sem.at[0], lin_sem.at[1], {"tensor": o})
    mod_copy = remote(mod_buf.at[c], mod_buf.at[c], mod_sem.at[0], mod_sem.at[1], {"tensor": o})

    lane = lax.broadcasted_iota(jnp.int32, (1, FREQ), 1)
    entry = jnp.where(lane < FREQ // 2, lane, lane - FREQ // 2).astype(F32)
    frequency = jnp.exp(-math.log(10000.0) * entry / (FREQ // 2))
    tick_rows = lax.broadcasted_iota(jnp.int32, (8, FREQ), 0)
    time_rows = jnp.zeros((8, FREQ), F32)
    for tick in range(TICKS):
        chosen = plan_ref[0, tick]
        time = jnp.int32(0)
        for micro in range(times_ref.shape[1]):
            time = time + jnp.where(chosen == micro, times_ref[0, micro], 0)
        time_rows = jnp.where(tick_rows == tick, time.astype(F32), time_rows)
    phases = time_rows * frequency
    embedded = jnp.where(lane < FREQ // 2, jnp.cos(phases), jnp.sin(phases))
    loads[1].wait()
    weights = mod_w[...]
    high = embedded.astype(BF16)
    rest = embedded - high.astype(F32)
    middle = rest.astype(BF16)
    low = (rest - middle.astype(F32)).astype(BF16)
    mod_buf[c] = (
        (dot_t(low, weights) + dot_t(middle, weights) + dot_t(high, weights))
        .astype(BF16)
        .astype(F32)
    )
    mod_copy.start()
    loads[0].wait()
    gate_cols[...] = mod_buf[c][:, half_width:].T
    mod_copy.wait()
    low_cols = mod_buf[0]
    high_cols = mod_buf[1]
    mod_full[0] = jnp.concatenate([low_cols[:, :half_width], high_cols[:, :half_width]], axis=1)
    mod_full[1] = jnp.concatenate([low_cols[:, half_width:], high_cols[:, half_width:]], axis=1)

    lin_copy.start()
    loads[2].wait()

    def skip_copy(tick):
        return remote(
            skip_out.at[tick],
            skip_in.at[tick],
            skip_send.at[tick],
            skip_recv.at[tick],
            {"section": mirror},
        )

    def x_copy(tick):
        return remote(
            y_out.at[tick],
            xin.at[tick + 1],
            x_send.at[tick],
            x_recv.at[tick],
            {"section": s + 1},
        )

    def x_wait(tick):
        remote(
            y_out.at[tick],
            xin.at[tick + 1],
            x_send.at[tick],
            x_recv.at[tick],
            {"section": s - 1},
        ).wait_recv()

    def linear(tick):
        return dot_t(xin[tick], lin_full[...].reshape(width, width))

    def fresh_arrive(tick):
        for block in range(half):

            @pl.when((c * half + block) > 0)
            def _():
                remote(
                    fresh_ref.at[tick],
                    fresh_in.at[tick, block],
                    fresh_send.at[tick],
                    fresh_recv.at[tick, block],
                    {"section": c * half + block},
                ).wait_recv()

        @pl.when(c == 0)
        def _():
            own_block = pltpu.make_async_copy(
                fresh_ref.at[tick], fresh_in.at[tick, 0], fresh_recv.at[tick, 0]
            )
            own_block.start()
            own_block.wait()

        xin[tick + 1] = fresh_in[tick].astype(F32).reshape(rows, width).astype(BF16)

    lane_head = lax.broadcasted_iota(jnp.int32, (rows, head_cols), 1)
    head_masks = [(lane_head >= DH * h) & (lane_head < DH * (h + 1)) for h in range(heads)]
    scale = 1.0 / math.sqrt(DH)

    def attend(part):
        q = q_buf[part]
        k = k_buf[...].reshape(2 * rows, head_cols)
        v = v_buf[...].reshape(2 * rows, head_cols)
        total = None
        for h in range(heads):
            q_h = jnp.where(head_masks[h], q, jnp.zeros_like(q))
            scores = (
                lax.dot_general(q_h, k, (((1,), (1,)), ((), ())), preferred_element_type=F32)
                * scale
            )
            top = jnp.max(scores, axis=-1, keepdims=True)
            grown = jnp.exp(scores - top)
            soft = (grown * (1.0 / jnp.sum(grown, axis=-1, keepdims=True))).astype(BF16)
            product = dot(soft, v)
            total = product if h == 0 else jnp.where(head_masks[h], product, total)
        return total.astype(BF16)

    def u_copy(tick):
        return remote(
            u_buf.at[tick, c], u_buf.at[tick, c], u_send.at[tick], u_recv.at[tick], {"tensor": o}
        )

    def u_wait(tick):
        remote(
            u_buf.at[tick, o], u_buf.at[tick, o], u_send.at[tick], u_recv.at[tick], {"tensor": o}
        ).wait_recv()

    def project(tick, part):
        rows_in = u_buf[tick, part]
        projected = dot_t(rows_in, qkv_ref[...]).astype(BF16)
        q_buf[part] = projected[:, :head_cols]
        k_buf[part] = projected[:, head_cols : 2 * head_cols]
        v_buf[part] = projected[:, 2 * head_cols :]

    def h_copy():
        return remote(h_cols.at[o], h_in, h_sem.at[0], h_sem.at[1], {"tensor": o})

    def block(tick):
        values = hidden[...]
        centred = values - jnp.mean(values, axis=-1, keepdims=True)
        variance = jnp.mean(centred * centred, axis=-1, keepdims=True)
        normed = centred * lax.rsqrt(variance + epsilon)
        scaling = mod_full[0, tick : tick + 1, :]
        u_buf[tick, c] = (normed * (1.0 + scaling)).astype(BF16)
        u_copy(tick).start()
        project(tick, c)
        if tick == last:
            turned = hidden[...].T
            h_cols[0] = turned[:half_width]
            h_cols[1] = turned[half_width:]
            h_copy().start()
        u_wait(tick)
        project(tick, o)

    def g_copy(tick):
        return remote(
            g_out.at[tick], g_in.at[tick], g_send.at[tick], g_recv.at[tick], {"tensor": o}
        )

    def relay(tick):
        g_out[tick] = dot(attend(o), out_w_ref[...]).astype(BF16)
        g_copy(tick).start()
        own = dot(attend(c), out_w_ref[...]).astype(BF16).astype(F32)
        gating = mod_full[1, tick : tick + 1, :]
        g_copy(tick).wait_recv()
        y = hidden[...] + gating * (own + g_in[tick].astype(F32))
        y_out[tick] = y.astype(BF16)
        x_copy(tick).start()

    def gl_copy(part):
        return remote(
            gl_out.at[part], gl_in.at[part], gl_send.at[part], gl_recv.at[part], {"tensor": o}
        )

    def settle():
        gating = gate_cols[:, last : last + 1]
        for part in range(2):
            heads_out = attend(part)
            gl_out[part] = dot_t(out_split[o], heads_out).astype(BF16)
            gl_copy(part).start()
            out_ref[:, part * rows : (part + 1) * rows] = (
                dot_t(out_split[c], heads_out).astype(BF16).astype(F32)
            )
        h_copy().wait_recv()
        for part in range(2):
            gl_copy(part).wait_recv()
            where = slice(part * rows, (part + 1) * rows)
            summed = out_ref[:, where] + gl_in[part].astype(F32)
            h_part = jnp.where(c == part, h_cols[c], h_in[...])
            out_ref[:, where] = h_part + gating * summed

    def skip_needed(tick):
        return down & (mirror <= sections - TICKS + tick)

    def send_skip(tick):
        skip_out[tick] = linear(tick).astype(BF16)
        skip_copy(tick).start()

    for tick in range(TICKS):
        live = s <= sections - TICKS + tick

        @pl.when((s > 0) & live)
        def _():
            if tick > 0:
                x_wait(tick - 1)

        if tick == 0:
            first_linear = skip_needed(0) | jnp.logical_not(down)

            @pl.when(first_linear)
            def _():
                loads[4].wait()
                lin_copy.wait()

        if tick > 0:

            @pl.when(skip_needed(tick) & (s > 0))
            def _():
                send_skip(tick)

        else:

            @pl.when(skip_needed(tick))
            def _():
                send_skip(tick)

        @pl.when(live & down)
        def _():
            hidden[...] = xin[tick].astype(F32)

        @pl.when(live & jnp.logical_not(down))
        def _():
            own = linear(tick)
            remote(
                skip_out.at[tick],
                skip_in.at[tick],
                skip_send.at[tick],
                skip_recv.at[tick],
                {"section": mirror},
            ).wait_recv()
            hidden[...] = own + skip_in[tick].astype(F32)

        if tick == 0:
            loads[3].wait()
            turned_out = out_w_ref[...].astype(F32).T.astype(BF16)
            out_split[0] = turned_out[:half_width]
            out_split[1] = turned_out[half_width:]

        if tick < last:

            @pl.when(live)
            def _():
                block(tick)
                relay(tick)

        else:
            block(tick)
            settle()

        if tick == 0:

            @pl.when(jnp.logical_not(first_linear))
            def _():
                loads[4].wait()
                lin_copy.wait()

            @pl.when(s == 0)
            def _():
                for later in reversed(range(TICKS - 1)):
                    fresh_arrive(later)
                for later in reversed(range(1, TICKS)):

                    @pl.when(skip_needed(later))
                    def _():
                        send_skip(later)

    @pl.when(fresh_sender)
    def _():
        for tick in range(TICKS - 1):
            fresh_copy(tick, s % half).wait_send()

    h_copy().wait_send()
    for part in range(2):
        gl_copy(part).wait_send()
    for tick in range(TICKS):

        @pl.when(skip_needed(tick))
        def _():
            skip_copy(tick).wait_send()

        @pl.when(s <= sections - TICKS + tick)
        def _():
            u_copy(tick).wait_send()
            if tick < last:
                g_copy(tick).wait_send()
                x_copy(tick).wait_send()


def on_device(inflow, fresh_rows, lin_weight, qkv_weight, out_weight, mod_weight, plan, timesteps):
    sections = lax.axis_size("section")
    row_count, width = inflow.shape[1:]
    rows = row_count // 2
    half_width = lin_weight.shape[2]
    head_cols = out_weight.shape[1]
    half = sections // 2
    piece = fresh_rows.shape[2]
    vmem = pl.BlockSpec(memory_space=pltpu.VMEM)
    hbm = pl.BlockSpec(memory_space=pltpu.HBM)
    smem = pl.BlockSpec(memory_space=pltpu.SMEM)
    dma = pltpu.SemaphoreType.DMA
    settled = pl.pallas_call(
        functools.partial(kernel, sections),
        out_shape=jax.ShapeDtypeStruct((half_width, row_count), F32),
        in_specs=[hbm] * 6 + [smem] * 2,
        out_specs=vmem,
        scratch_shapes=[
            pltpu.VMEM((3 * head_cols, width), BF16),
            pltpu.VMEM((head_cols, width), BF16),
            pltpu.VMEM((2 * half_width, FREQ), BF16),
            dma((5,)),
            pltpu.VMEM((2, half_width, width), BF16),
            pltpu.VMEM((2, half_width, head_cols), BF16),
            pltpu.VMEM((2, 8, 2 * half_width), F32),
            pltpu.VMEM((2, 8, width), F32),
            pltpu.VMEM((half_width, 8), F32),
            pltpu.VMEM((TICKS - 1, half, piece, width), BF16),
            pltpu.VMEM((TICKS, rows, width), BF16),
            pltpu.VMEM((TICKS, rows, width), BF16),
            pltpu.VMEM((TICKS, rows, width), BF16),
            pltpu.VMEM((rows, width), F32),
            pltpu.VMEM((TICKS, 2, rows, width), BF16),
            pltpu.VMEM((2, rows, head_cols), BF16),
            pltpu.VMEM((2, rows, head_cols), BF16),
            pltpu.VMEM((2, rows, head_cols), BF16),
            pltpu.VMEM((TICKS - 1, rows, width), BF16),
            pltpu.VMEM((TICKS - 1, rows, width), BF16),
            pltpu.VMEM((2, half_width, rows), BF16),
            pltpu.VMEM((2, half_width, rows), BF16),
            pltpu.VMEM((2, half_width, rows), F32),
            pltpu.VMEM((half_width, rows), F32),
            pltpu.VMEM((TICKS - 1, rows, width), BF16),
            dma((2,)),
            dma((2,)),
            dma((TICKS - 1,)),
            dma((TICKS - 1, half)),
            dma((TICKS - 1,)),
            dma((TICKS - 1,)),
            dma((TICKS,)),
            dma((TICKS,)),
            dma((TICKS,)),
            dma((TICKS,)),
            dma((TICKS - 1,)),
            dma((TICKS - 1,)),
            dma((2,)),
            dma((2,)),
            dma((2,)),
        ],
        compiler_params=pltpu.CompilerParams(
            collective_id=0, has_side_effects=True, vmem_limit_bytes=63 * 2**20
        ),
    )(
        inflow[0].reshape(2, rows, width),
        fresh_rows[:, 0],
        lin_weight[0].T,
        qkv_weight[0].transpose(0, 2, 1).reshape(3 * head_cols, width),
        out_weight[0],
        mod_weight[0].transpose(1, 2, 0).reshape(2 * half_width, FREQ),
        plan.T,
        timesteps.T,
    )
    return settled.T[None]


def solution(mesh):
    return jax.shard_map(
        on_device,
        mesh=mesh,
        in_specs=(
            P("section", ("groups", "replica"), None),
            P(None, ("groups", "replica"), "section", None),
            P("section", None, "tensor"),
            P("section", None, None, "tensor"),
            P("section", "tensor", None),
            P("section", None, None, "tensor"),
            P(None, "section"),
            P(None, ("groups", "replica")),
        ),
        out_specs=P("section", ("groups", "replica"), "tensor"),
        check_vma=False,
    )
```

```python
import functools
import math

import jax
import jax.numpy as jnp
from jax import lax
from jax.experimental import pallas as pl
from jax.experimental.pallas import tpu as pltpu
from jax.sharding import PartitionSpec as P

DH = 72
FREQ = 128
TICKS = 3
epsilon = 1e-06
F32 = jnp.float32
BF16 = jnp.bfloat16


def dot(a, b):
    return jnp.dot(a, b, preferred_element_type=F32)


def dot_t(a, b):
    return lax.dot_general(a, b, (((1,), (1,)), ((), ())), preferred_element_type=F32)


def kernel(
    sections,
    inflow_hbm,
    fresh_ref,
    lin_ref,
    qkv_hbm,
    out_w_hbm,
    mod_hbm,
    plan_ref,
    times_ref,
    out_ref,
    qkv_ref,
    out_w_ref,
    mod_w,
    load_sem,
    lin_full,
    out_split,
    mod_buf,
    mod_full,
    gate_cols,
    fresh_in,
    xin,
    skip_out,
    skip_in,
    hidden,
    u_buf,
    q_buf,
    k_buf,
    v_buf,
    g_out,
    g_in,
    gl_out,
    gl_in,
    h_cols,
    h_in,
    y_out,
    lin_sem,
    mod_sem,
    fresh_send,
    fresh_recv,
    x_send,
    x_recv,
    skip_send,
    skip_recv,
    u_send,
    u_recv,
    g_send,
    g_recv,
    gl_send,
    gl_recv,
    h_sem,
):
    s = lax.axis_index("section")
    c = lax.axis_index("tensor")
    o = 1 - c
    half = sections // 2
    mirror = sections - 1 - s
    down = s < half
    rows = inflow_hbm.shape[1]
    width = inflow_hbm.shape[2]
    half_width = width // 2
    heads = out_w_ref.shape[0] // DH
    head_cols = out_w_ref.shape[0]
    last = TICKS - 1

    loads = [
        pltpu.make_async_copy(inflow_hbm.at[c], xin.at[0], load_sem.at[0]),
        pltpu.make_async_copy(mod_hbm, mod_w, load_sem.at[1]),
        pltpu.make_async_copy(qkv_hbm, qkv_ref, load_sem.at[2]),
        pltpu.make_async_copy(out_w_hbm, out_w_ref, load_sem.at[3]),
        pltpu.make_async_copy(lin_ref, lin_full.at[c], load_sem.at[4]),
    ]
    for load in loads:
        load.start()

    def remote(src, dst, send, recv, device):
        return pltpu.make_async_remote_copy(
            src_ref=src,
            dst_ref=dst,
            send_sem=send,
            recv_sem=recv,
            device_id=device,
            device_id_type=pl.DeviceIdType.MESH,
        )

    fresh_sender = (s > 0) & (s // half == c)

    barrier = pltpu.get_barrier_semaphore()

    def greet(device):
        pl.semaphore_signal(
            barrier, inc=1, device_id=device, device_id_type=pl.DeviceIdType.MESH
        )

    greet({"tensor": o})
    greet({"section": mirror})

    @pl.when(s > 0)
    def _():
        greet({"section": s - 1})

    @pl.when(s < sections - 1)
    def _():
        greet({"section": s + 1})

    @pl.when(fresh_sender)
    def _():
        greet({"section": 0})

    @pl.when(s == 0)
    def _():
        for block in range(half):

            @pl.when((c * half + block) > 0)
            def _():
                greet({"section": c * half + block})

    expected = (
        2
        + jnp.where(s > 0, 1, 0)
        + jnp.where(s < sections - 1, 1, 0)
        + jnp.where(fresh_sender, 1, 0)
        + jnp.where(s == 0, half - 1 + c, 0)
    )
    pl.semaphore_wait(barrier, expected)

    def fresh_copy(tick, block):
        return remote(
            fresh_ref.at[tick],
            fresh_in.at[tick, block],
            fresh_send.at[tick],
            fresh_recv.at[tick, block],
            {"section": 0},
        )

    @pl.when(fresh_sender)
    def _():
        for tick in range(TICKS - 1):
            fresh_copy(tick, s % half).start()

    lin_copy = remote(lin_ref, lin_full.at[c], lin_sem.at[0], lin_sem.at[1], {"tensor": o})
    mod_copy = remote(mod_buf.at[c], mod_buf.at[c], mod_sem.at[0], mod_sem.at[1], {"tensor": o})

    lane = lax.broadcasted_iota(jnp.int32, (1, FREQ), 1)
    entry = jnp.where(lane < FREQ // 2, lane, lane - FREQ // 2).astype(F32)
    frequency = jnp.exp(-math.log(10000.0) * entry / (FREQ // 2))
    tick_rows = lax.broadcasted_iota(jnp.int32, (8, FREQ), 0)
    time_rows = jnp.zeros((8, FREQ), F32)
    for tick in range(TICKS):
        chosen = plan_ref[0, tick]
        time = jnp.int32(0)
        for micro in range(times_ref.shape[1]):
            time = time + jnp.where(chosen == micro, times_ref[0, micro], 0)
        time_rows = jnp.where(tick_rows == tick, time.astype(F32), time_rows)
    phases = time_rows * frequency
    embedded = jnp.where(lane < FREQ // 2, jnp.cos(phases), jnp.sin(phases))
    loads[1].wait()
    weights = mod_w[...]
    high = embedded.astype(BF16)
    rest = embedded - high.astype(F32)
    middle = rest.astype(BF16)
    low = (rest - middle.astype(F32)).astype(BF16)
    mod_buf[c] = (
        (dot_t(low, weights) + dot_t(middle, weights) + dot_t(high, weights))
        .astype(BF16)
        .astype(F32)
    )
    mod_copy.start()
    loads[0].wait()
    gate_cols[...] = mod_buf[c][:, half_width:].T
    mod_copy.wait()
    low_cols = mod_buf[0]
    high_cols = mod_buf[1]
    mod_full[0] = jnp.concatenate([low_cols[:, :half_width], high_cols[:, :half_width]], axis=1)
    mod_full[1] = jnp.concatenate([low_cols[:, half_width:], high_cols[:, half_width:]], axis=1)

    lin_copy.start()
    loads[2].wait()

    def skip_copy(tick):
        return remote(
            skip_out.at[tick],
            skip_in.at[tick],
            skip_send.at[tick],
            skip_recv.at[tick],
            {"section": mirror},
        )

    def x_copy(tick):
        return remote(
            y_out.at[tick],
            xin.at[tick + 1],
            x_send.at[tick],
            x_recv.at[tick],
            {"section": s + 1},
        )

    def x_wait(tick):
        remote(
            y_out.at[tick],
            xin.at[tick + 1],
            x_send.at[tick],
            x_recv.at[tick],
            {"section": s - 1},
        ).wait_recv()

    def linear(tick):
        return dot_t(xin[tick], lin_full[...].reshape(width, width))

    def fresh_arrive(tick):
        for block in range(half):

            @pl.when((c * half + block) > 0)
            def _():
                remote(
                    fresh_ref.at[tick],
                    fresh_in.at[tick, block],
                    fresh_send.at[tick],
                    fresh_recv.at[tick, block],
                    {"section": c * half + block},
                ).wait_recv()

        @pl.when(c == 0)
        def _():
            own_block = pltpu.make_async_copy(
                fresh_ref.at[tick], fresh_in.at[tick, 0], fresh_recv.at[tick, 0]
            )
            own_block.start()
            own_block.wait()

        xin[tick + 1] = fresh_in[tick].astype(F32).reshape(rows, width).astype(BF16)

    lane_head = lax.broadcasted_iota(jnp.int32, (rows, head_cols), 1)
    head_masks = [(lane_head >= DH * h) & (lane_head < DH * (h + 1)) for h in range(heads)]
    scale = 1.0 / math.sqrt(DH)

    def attend(part):
        q = q_buf[part]
        k = k_buf[...].reshape(2 * rows, head_cols)
        v = v_buf[...].reshape(2 * rows, head_cols)
        total = None
        for h in range(heads):
            q_h = jnp.where(head_masks[h], q, jnp.zeros_like(q))
            scores = (
                lax.dot_general(q_h, k, (((1,), (1,)), ((), ())), preferred_element_type=F32)
                * scale
            )
            top = jnp.max(scores, axis=-1, keepdims=True)
            grown = jnp.exp(scores - top)
            soft = (grown * (1.0 / jnp.sum(grown, axis=-1, keepdims=True))).astype(BF16)
            product = dot(soft, v)
            total = product if h == 0 else jnp.where(head_masks[h], product, total)
        return total.astype(BF16)

    def u_copy(tick):
        return remote(
            u_buf.at[tick, c], u_buf.at[tick, c], u_send.at[tick], u_recv.at[tick], {"tensor": o}
        )

    def u_wait(tick):
        remote(
            u_buf.at[tick, o], u_buf.at[tick, o], u_send.at[tick], u_recv.at[tick], {"tensor": o}
        ).wait_recv()

    def project(tick, part):
        rows_in = u_buf[tick, part]
        projected = dot_t(rows_in, qkv_ref[...]).astype(BF16)
        q_buf[part] = projected[:, :head_cols]
        k_buf[part] = projected[:, head_cols : 2 * head_cols]
        v_buf[part] = projected[:, 2 * head_cols :]

    def h_copy():
        return remote(h_cols.at[o], h_in, h_sem.at[0], h_sem.at[1], {"tensor": o})

    def block(tick):
        values = hidden[...]
        centred = values - jnp.mean(values, axis=-1, keepdims=True)
        variance = jnp.mean(centred * centred, axis=-1, keepdims=True)
        normed = centred * lax.rsqrt(variance + epsilon)
        scaling = mod_full[0, tick : tick + 1, :]
        u_buf[tick, c] = (normed * (1.0 + scaling)).astype(BF16)
        u_copy(tick).start()
        project(tick, c)
        if tick == last:
            turned = hidden[...].T
            h_cols[0] = turned[:half_width]
            h_cols[1] = turned[half_width:]
            h_copy().start()
        u_wait(tick)
        project(tick, o)

    def g_copy(tick):
        return remote(
            g_out.at[tick], g_in.at[tick], g_send.at[tick], g_recv.at[tick], {"tensor": o}
        )

    def relay(tick):
        g_out[tick] = dot(attend(o), out_w_ref[...]).astype(BF16)
        g_copy(tick).start()
        own = dot(attend(c), out_w_ref[...]).astype(BF16).astype(F32)
        gating = mod_full[1, tick : tick + 1, :]
        g_copy(tick).wait_recv()
        y = hidden[...] + gating * (own + g_in[tick].astype(F32))
        y_out[tick] = y.astype(BF16)
        x_copy(tick).start()

    def gl_copy(part):
        return remote(
            gl_out.at[part], gl_in.at[part], gl_send.at[part], gl_recv.at[part], {"tensor": o}
        )

    def settle():
        gating = gate_cols[:, last : last + 1]
        for part in range(2):
            heads_out = attend(part)
            gl_out[part] = dot_t(out_split[o], heads_out).astype(BF16)
            gl_copy(part).start()
            out_ref[:, part * rows : (part + 1) * rows] = (
                dot_t(out_split[c], heads_out).astype(BF16).astype(F32)
            )
        h_copy().wait_recv()
        for part in range(2):
            gl_copy(part).wait_recv()
            where = slice(part * rows, (part + 1) * rows)
            summed = out_ref[:, where] + gl_in[part].astype(F32)
            h_part = jnp.where(c == part, h_cols[c], h_in[...])
            out_ref[:, where] = h_part + gating * summed

    def skip_needed(tick):
        return down & (mirror <= sections - TICKS + tick)

    def send_skip(tick):
        skip_out[tick] = linear(tick).astype(BF16)
        skip_copy(tick).start()

    for tick in range(TICKS):
        live = s <= sections - TICKS + tick

        @pl.when((s > 0) & live)
        def _():
            if tick > 0:
                x_wait(tick - 1)

        if tick == 0:
            first_linear = skip_needed(0) | jnp.logical_not(down)

            @pl.when(first_linear)
            def _():
                loads[4].wait()
                lin_copy.wait()

        if tick == last:
            @pl.when(s == 0)
            def _():
                x_copy(last - 1).wait_send()

        @pl.when(skip_needed(tick))
        def _():
            send_skip(tick)

        @pl.when(live & down)
        def _():
            hidden[...] = xin[tick].astype(F32)

        @pl.when(live & jnp.logical_not(down))
        def _():
            own = linear(tick)
            remote(
                skip_out.at[tick],
                skip_in.at[tick],
                skip_send.at[tick],
                skip_recv.at[tick],
                {"section": mirror},
            ).wait_recv()
            hidden[...] = own + skip_in[tick].astype(F32)

        if tick == 0:
            loads[3].wait()
            turned_out = out_w_ref[...].astype(F32).T.astype(BF16)
            out_split[0] = turned_out[:half_width]
            out_split[1] = turned_out[half_width:]

        if tick < last:

            @pl.when(live)
            def _():
                block(tick)
                relay(tick)

        else:
            block(tick)
            settle()

        if tick == 0:

            @pl.when(jnp.logical_not(first_linear))
            def _():
                loads[4].wait()
                lin_copy.wait()

            @pl.when(s == 0)
            def _():
                for later in range(TICKS - 1):
                    fresh_arrive(later)

    @pl.when(fresh_sender)
    def _():
        for tick in range(TICKS - 1):
            fresh_copy(tick, s % half).wait_send()

    h_copy().wait_send()
    for part in range(2):
        gl_copy(part).wait_send()
    for tick in range(TICKS):

        @pl.when(skip_needed(tick))
        def _():
            skip_copy(tick).wait_send()

        @pl.when(s <= sections - TICKS + tick)
        def _():
            u_copy(tick).wait_send()
            if tick < last:
                g_copy(tick).wait_send()
                if tick < last - 1:
                    x_copy(tick).wait_send()
                else:

                    @pl.when(s > 0)
                    def _():
                        x_copy(tick).wait_send()


def on_device(inflow, fresh_rows, lin_weight, qkv_weight, out_weight, mod_weight, plan, timesteps):
    sections = lax.axis_size("section")
    row_count, width = inflow.shape[1:]
    rows = row_count // 2
    half_width = lin_weight.shape[2]
    head_cols = out_weight.shape[1]
    half = sections // 2
    piece = fresh_rows.shape[2]
    vmem = pl.BlockSpec(memory_space=pltpu.VMEM)
    hbm = pl.BlockSpec(memory_space=pltpu.HBM)
    smem = pl.BlockSpec(memory_space=pltpu.SMEM)
    dma = pltpu.SemaphoreType.DMA
    settled = pl.pallas_call(
        functools.partial(kernel, sections),
        out_shape=jax.ShapeDtypeStruct((half_width, row_count), F32),
        in_specs=[hbm] * 6 + [smem] * 2,
        out_specs=vmem,
        scratch_shapes=[
            pltpu.VMEM((3 * head_cols, width), BF16),
            pltpu.VMEM((head_cols, width), BF16),
            pltpu.VMEM((2 * half_width, FREQ), BF16),
            dma((5,)),
            pltpu.VMEM((2, half_width, width), BF16),
            pltpu.VMEM((2, half_width, head_cols), BF16),
            pltpu.VMEM((2, 8, 2 * half_width), F32),
            pltpu.VMEM((2, 8, width), F32),
            pltpu.VMEM((half_width, 8), F32),
            pltpu.VMEM((TICKS - 1, half, piece, width), BF16),
            pltpu.VMEM((TICKS, rows, width), BF16),
            pltpu.VMEM((TICKS, rows, width), BF16),
            pltpu.VMEM((TICKS, rows, width), BF16),
            pltpu.VMEM((rows, width), F32),
            pltpu.VMEM((TICKS, 2, rows, width), BF16),
            pltpu.VMEM((2, rows, head_cols), BF16),
            pltpu.VMEM((2, rows, head_cols), BF16),
            pltpu.VMEM((2, rows, head_cols), BF16),
            pltpu.VMEM((TICKS - 1, rows, width), BF16),
            pltpu.VMEM((TICKS - 1, rows, width), BF16),
            pltpu.VMEM((2, half_width, rows), BF16),
            pltpu.VMEM((2, half_width, rows), BF16),
            pltpu.VMEM((2, half_width, rows), F32),
            pltpu.VMEM((half_width, rows), F32),
            pltpu.VMEM((TICKS - 1, rows, width), BF16),
            dma((2,)),
            dma((2,)),
            dma((TICKS - 1,)),
            dma((TICKS - 1, half)),
            dma((TICKS - 1,)),
            dma((TICKS - 1,)),
            dma((TICKS,)),
            dma((TICKS,)),
            dma((TICKS,)),
            dma((TICKS,)),
            dma((TICKS - 1,)),
            dma((TICKS - 1,)),
            dma((2,)),
            dma((2,)),
            dma((2,)),
        ],
        compiler_params=pltpu.CompilerParams(
            collective_id=0, has_side_effects=True, vmem_limit_bytes=62 * 2**20 + 2**18
        ),
    )(
        inflow[0].reshape(2, rows, width),
        fresh_rows[:, 0],
        lin_weight[0].T,
        qkv_weight[0].transpose(0, 2, 1).reshape(3 * head_cols, width),
        out_weight[0],
        mod_weight[0].transpose(1, 2, 0).reshape(2 * half_width, FREQ),
        plan.T,
        timesteps.T,
    )
    return settled.T[None]


def solution(mesh):
    return jax.shard_map(
        on_device,
        mesh=mesh,
        in_specs=(
            P("section", ("groups", "replica"), None),
            P(None, ("groups", "replica"), "section", None),
            P("section", None, "tensor"),
            P("section", None, None, "tensor"),
            P("section", "tensor", None),
            P("section", None, None, "tensor"),
            P(None, "section"),
            P(None, ("groups", "replica")),
        ),
        out_specs=P("section", ("groups", "replica"), "tensor"),
        check_vma=False,
    )
```

```python
import functools
import math

import jax
import jax.numpy as jnp
from jax import lax
from jax.experimental import pallas as pl
from jax.experimental.pallas import tpu as pltpu
from jax.sharding import PartitionSpec as P

DH = 72
FREQ = 128
TICKS = 3
epsilon = 1e-06
F32 = jnp.float32
BF16 = jnp.bfloat16


def dot(a, b):
    return jnp.dot(a, b, preferred_element_type=F32)


def dot_t(a, b):
    return lax.dot_general(a, b, (((1,), (1,)), ((), ())), preferred_element_type=F32)


def kernel(
    sections,
    inflow_hbm,
    fresh_ref,
    lin_ref,
    qkv_hbm,
    out_w_hbm,
    mod_hbm,
    plan_ref,
    times_ref,
    out_ref,
    qkv_ref,
    out_w_ref,
    mod_w,
    load_sem,
    lin_full,
    out_split,
    mod_buf,
    mod_full,
    gate_cols,
    fresh_in,
    xin,
    skip_out,
    skip_in,
    hidden,
    u_buf,
    q_buf,
    k_buf,
    v_buf,
    g_out,
    g_in,
    gl_out,
    gl_in,
    h_cols,
    h_in,
    y_out,
    lin_sem,
    mod_sem,
    fresh_send,
    fresh_recv,
    x_send,
    x_recv,
    skip_send,
    skip_recv,
    u_send,
    u_recv,
    g_send,
    g_recv,
    gl_send,
    gl_recv,
    h_sem,
):
    s = lax.axis_index("section")
    c = lax.axis_index("tensor")
    o = 1 - c
    half = sections // 2
    mirror = sections - 1 - s
    down = s < half
    rows = inflow_hbm.shape[1]
    width = inflow_hbm.shape[2]
    half_width = width // 2
    heads = out_w_ref.shape[0] // DH
    head_cols = out_w_ref.shape[0]
    last = TICKS - 1

    loads = [
        pltpu.make_async_copy(inflow_hbm.at[c], xin.at[0], load_sem.at[0]),
        pltpu.make_async_copy(mod_hbm, mod_w, load_sem.at[1]),
        pltpu.make_async_copy(qkv_hbm, qkv_ref, load_sem.at[2]),
        pltpu.make_async_copy(out_w_hbm, out_w_ref, load_sem.at[3]),
        pltpu.make_async_copy(lin_ref, lin_full.at[c], load_sem.at[4]),
    ]
    for load in loads:
        load.start()

    def remote(src, dst, send, recv, device):
        return pltpu.make_async_remote_copy(
            src_ref=src,
            dst_ref=dst,
            send_sem=send,
            recv_sem=recv,
            device_id=device,
            device_id_type=pl.DeviceIdType.MESH,
        )

    fresh_sender = (s > 0) & (s // half == c)

    barrier = pltpu.get_barrier_semaphore()

    def greet(device):
        pl.semaphore_signal(
            barrier, inc=1, device_id=device, device_id_type=pl.DeviceIdType.MESH
        )

    greet({"tensor": o})
    greet({"section": mirror})

    @pl.when(s > 0)
    def _():
        greet({"section": s - 1})

    @pl.when(s < sections - 1)
    def _():
        greet({"section": s + 1})

    @pl.when(fresh_sender)
    def _():
        greet({"section": 0})

    @pl.when(s == 0)
    def _():
        for block in range(half):

            @pl.when((c * half + block) > 0)
            def _():
                greet({"section": c * half + block})

    expected = (
        2
        + jnp.where(s > 0, 1, 0)
        + jnp.where(s < sections - 1, 1, 0)
        + jnp.where(fresh_sender, 1, 0)
        + jnp.where(s == 0, half - 1 + c, 0)
    )
    pl.semaphore_wait(barrier, expected)

    def fresh_copy(tick, block):
        return remote(
            fresh_ref.at[tick],
            fresh_in.at[tick, block],
            fresh_send.at[tick],
            fresh_recv.at[tick, block],
            {"section": 0},
        )

    @pl.when(fresh_sender)
    def _():
        for tick in range(TICKS - 1):
            fresh_copy(tick, s % half).start()

    lin_copy = remote(lin_ref, lin_full.at[c], lin_sem.at[0], lin_sem.at[1], {"tensor": o})
    mod_copy = remote(mod_buf.at[c], mod_buf.at[c], mod_sem.at[0], mod_sem.at[1], {"tensor": o})

    lane = lax.broadcasted_iota(jnp.int32, (1, FREQ), 1)
    entry = jnp.where(lane < FREQ // 2, lane, lane - FREQ // 2).astype(F32)
    frequency = jnp.exp(-math.log(10000.0) * entry / (FREQ // 2))
    tick_rows = lax.broadcasted_iota(jnp.int32, (8, FREQ), 0)
    time_rows = jnp.zeros((8, FREQ), F32)
    for tick in range(TICKS):
        chosen = plan_ref[0, tick]
        time = jnp.int32(0)
        for micro in range(times_ref.shape[1]):
            time = time + jnp.where(chosen == micro, times_ref[0, micro], 0)
        time_rows = jnp.where(tick_rows == tick, time.astype(F32), time_rows)
    phases = time_rows * frequency
    embedded = jnp.where(lane < FREQ // 2, jnp.cos(phases), jnp.sin(phases))
    loads[1].wait()
    weights = mod_w[...]
    high = embedded.astype(BF16)
    rest = embedded - high.astype(F32)
    middle = rest.astype(BF16)
    low = (rest - middle.astype(F32)).astype(BF16)
    mod_buf[c] = (
        (dot_t(low, weights) + dot_t(middle, weights) + dot_t(high, weights))
        .astype(BF16)
        .astype(F32)
    )
    mod_copy.start()
    loads[0].wait()
    mod_copy.wait()
    low_cols = mod_buf[0]
    high_cols = mod_buf[1]
    mod_full[0] = jnp.concatenate([low_cols[:, :half_width], high_cols[:, :half_width]], axis=1)
    mod_full[1] = jnp.concatenate([low_cols[:, half_width:], high_cols[:, half_width:]], axis=1)

    loads[2].wait()

    def skip_copy(tick):
        return remote(
            skip_out.at[tick],
            skip_in.at[tick],
            skip_send.at[tick],
            skip_recv.at[tick],
            {"section": mirror},
        )

    def x_copy(tick):
        return remote(
            y_out.at[tick],
            xin.at[tick + 1],
            x_send.at[tick],
            x_recv.at[tick],
            {"section": s + 1},
        )

    def x_wait(tick):
        remote(
            y_out.at[tick],
            xin.at[tick + 1],
            x_send.at[tick],
            x_recv.at[tick],
            {"section": s - 1},
        ).wait_recv()

    def linear(tick):
        return dot_t(xin[tick], lin_full[...].reshape(width, width))

    def fresh_arrive(tick):
        for block in range(half):

            @pl.when((c * half + block) > 0)
            def _():
                remote(
                    fresh_ref.at[tick],
                    fresh_in.at[tick, block],
                    fresh_send.at[tick],
                    fresh_recv.at[tick, block],
                    {"section": c * half + block},
                ).wait_recv()

        @pl.when(c == 0)
        def _():
            own_block = pltpu.make_async_copy(
                fresh_ref.at[tick], fresh_in.at[tick, 0], fresh_recv.at[tick, 0]
            )
            own_block.start()
            own_block.wait()

        xin[tick + 1] = fresh_in[tick].astype(F32).reshape(rows, width).astype(BF16)

    lane_head = lax.broadcasted_iota(jnp.int32, (rows, head_cols), 1)
    head_masks = [(lane_head >= DH * h) & (lane_head < DH * (h + 1)) for h in range(heads)]
    scale = 1.0 / math.sqrt(DH)

    def attend(part):
        q = q_buf[part]
        k = k_buf[...].reshape(2 * rows, head_cols)
        v = v_buf[...].reshape(2 * rows, head_cols)
        total = None
        for h in range(heads):
            q_h = jnp.where(head_masks[h], q, jnp.zeros_like(q))
            scores = (
                lax.dot_general(q_h, k, (((1,), (1,)), ((), ())), preferred_element_type=F32)
                * scale
            )
            top = jnp.max(scores, axis=-1, keepdims=True)
            grown = jnp.exp(scores - top)
            soft = (grown * (1.0 / jnp.sum(grown, axis=-1, keepdims=True))).astype(BF16)
            product = dot(soft, v)
            total = product if h == 0 else jnp.where(head_masks[h], product, total)
        return total.astype(BF16)

    def u_copy(tick):
        return remote(
            u_buf.at[tick, c], u_buf.at[tick, c], u_send.at[tick], u_recv.at[tick], {"tensor": o}
        )

    def u_wait(tick):
        remote(
            u_buf.at[tick, o], u_buf.at[tick, o], u_send.at[tick], u_recv.at[tick], {"tensor": o}
        ).wait_recv()

    def project(tick, part):
        rows_in = u_buf[tick, part]
        projected = dot_t(rows_in, qkv_ref[...]).astype(BF16)
        q_buf[part] = projected[:, :head_cols]
        k_buf[part] = projected[:, head_cols : 2 * head_cols]
        v_buf[part] = projected[:, 2 * head_cols :]

    def h_copy():
        return remote(h_cols.at[o], h_in, h_sem.at[0], h_sem.at[1], {"tensor": o})

    def block(tick):
        values = hidden[...]
        centred = values - jnp.mean(values, axis=-1, keepdims=True)
        variance = jnp.mean(centred * centred, axis=-1, keepdims=True)
        normed = centred * lax.rsqrt(variance + epsilon)
        scaling = mod_full[0, tick : tick + 1, :]
        u_buf[tick, c] = (normed * (1.0 + scaling)).astype(BF16)
        u_copy(tick).start()
        project(tick, c)
        if tick == last:
            turned = hidden[...].T
            h_cols[0] = turned[:half_width]
            h_cols[1] = turned[half_width:]
            h_copy().start()
        u_wait(tick)
        project(tick, o)

    def g_copy(tick):
        return remote(
            g_out.at[tick], g_in.at[tick], g_send.at[tick], g_recv.at[tick], {"tensor": o}
        )

    def relay(tick):
        g_out[tick] = dot(attend(o), out_w_ref[...]).astype(BF16)
        g_copy(tick).start()
        own = dot(attend(c), out_w_ref[...]).astype(BF16).astype(F32)
        gating = mod_full[1, tick : tick + 1, :]
        g_copy(tick).wait_recv()
        y = hidden[...] + gating * (own + g_in[tick].astype(F32))
        y_out[tick] = y.astype(BF16)
        x_copy(tick).start()

    def gl_copy(part):
        return remote(
            gl_out.at[part], gl_in.at[part], gl_send.at[part], gl_recv.at[part], {"tensor": o}
        )

    def settle():
        gating = gate_cols[:, last : last + 1]
        for part in range(2):
            heads_out = attend(part)
            gl_out[part] = dot_t(out_split[o], heads_out).astype(BF16)
            gl_copy(part).start()
            out_ref[:, part * rows : (part + 1) * rows] = (
                dot_t(out_split[c], heads_out).astype(BF16).astype(F32)
            )
        h_copy().wait_recv()
        for part in range(2):
            gl_copy(part).wait_recv()
            where = slice(part * rows, (part + 1) * rows)
            summed = out_ref[:, where] + gl_in[part].astype(F32)
            h_part = jnp.where(c == part, h_cols[c], h_in[...])
            out_ref[:, where] = h_part + gating * summed

    def skip_needed(tick):
        return down & (mirror <= sections - TICKS + tick)

    def send_skip(tick):
        skip_out[tick] = linear(tick).astype(BF16)
        skip_copy(tick).start()

    for tick in range(TICKS):
        live = s <= sections - TICKS + tick

        @pl.when((s > 0) & live)
        def _():
            if tick > 0:
                x_wait(tick - 1)

        if tick == 0:
            first_linear = skip_needed(0) | (jnp.logical_not(down) & live)

            @pl.when(first_linear)
            def _():
                lin_copy.start()
                loads[4].wait()
                lin_copy.wait()

        if tick == 1:

            @pl.when(jnp.logical_not(first_linear) & (s > 0))
            def _():
                loads[4].wait()
                lin_copy.wait()

        @pl.when(skip_needed(tick) & (s > 0))
        def _():
            send_skip(tick)

        @pl.when(live & down)
        def _():
            hidden[...] = xin[tick].astype(F32)

        @pl.when(live & jnp.logical_not(down))
        def _():
            own = linear(tick)
            remote(
                skip_out.at[tick],
                skip_in.at[tick],
                skip_send.at[tick],
                skip_recv.at[tick],
                {"section": mirror},
            ).wait_recv()
            hidden[...] = own + skip_in[tick].astype(F32)

        if tick == 0:
            loads[3].wait()

        if tick < last:

            @pl.when(live)
            def _():
                block(tick)
                if tick == last - 1:
                    @pl.when(s == 0)
                    def _():
                        loads[4].wait()
                        lin_copy.wait()
                        x_copy(0).wait_send()
                        send_skip(last)

                relay(tick)

        else:
            block(tick)
            settle()

        if tick == 0:

            @pl.when(jnp.logical_not(first_linear))
            def _():
                lin_copy.start()

            turned_out = out_w_ref[...].astype(F32).T.astype(BF16)
            out_split[0] = turned_out[:half_width]
            out_split[1] = turned_out[half_width:]
            gate_cols[...] = mod_buf[c][:, half_width:].T

            @pl.when(s == 0)
            def _():
                for later in range(TICKS - 1):
                    fresh_arrive(later)

    @pl.when(fresh_sender)
    def _():
        for tick in range(TICKS - 1):
            fresh_copy(tick, s % half).wait_send()

    h_copy().wait_send()
    for part in range(2):
        gl_copy(part).wait_send()
    for tick in range(TICKS):

        @pl.when(skip_needed(tick))
        def _():
            skip_copy(tick).wait_send()

        @pl.when(s <= sections - TICKS + tick)
        def _():
            u_copy(tick).wait_send()
            if tick < last:
                g_copy(tick).wait_send()
                if tick > 0:
                    x_copy(tick).wait_send()
                else:

                    @pl.when(s > 0)
                    def _():
                        x_copy(tick).wait_send()


def on_device(inflow, fresh_rows, lin_weight, qkv_weight, out_weight, mod_weight, plan, timesteps):
    sections = lax.axis_size("section")
    row_count, width = inflow.shape[1:]
    rows = row_count // 2
    half_width = lin_weight.shape[2]
    head_cols = out_weight.shape[1]
    half = sections // 2
    piece = fresh_rows.shape[2]
    vmem = pl.BlockSpec(memory_space=pltpu.VMEM)
    hbm = pl.BlockSpec(memory_space=pltpu.HBM)
    smem = pl.BlockSpec(memory_space=pltpu.SMEM)
    dma = pltpu.SemaphoreType.DMA
    settled = pl.pallas_call(
        functools.partial(kernel, sections),
        out_shape=jax.ShapeDtypeStruct((half_width, row_count), F32),
        in_specs=[hbm] * 6 + [smem] * 2,
        out_specs=vmem,
        scratch_shapes=[
            pltpu.VMEM((3 * head_cols, width), BF16),
            pltpu.VMEM((head_cols, width), BF16),
            pltpu.VMEM((2 * half_width, FREQ), BF16),
            dma((5,)),
            pltpu.VMEM((2, half_width, width), BF16),
            pltpu.VMEM((2, half_width, head_cols), BF16),
            pltpu.VMEM((2, 8, 2 * half_width), F32),
            pltpu.VMEM((2, 8, width), F32),
            pltpu.VMEM((half_width, 8), F32),
            pltpu.VMEM((TICKS - 1, half, piece, width), BF16),
            pltpu.VMEM((TICKS, rows, width), BF16),
            pltpu.VMEM((TICKS, rows, width), BF16),
            pltpu.VMEM((TICKS, rows, width), BF16),
            pltpu.VMEM((rows, width), F32),
            pltpu.VMEM((TICKS, 2, rows, width), BF16),
            pltpu.VMEM((2, rows, head_cols), BF16),
            pltpu.VMEM((2, rows, head_cols), BF16),
            pltpu.VMEM((2, rows, head_cols), BF16),
            pltpu.VMEM((TICKS - 1, rows, width), BF16),
            pltpu.VMEM((TICKS - 1, rows, width), BF16),
            pltpu.VMEM((2, half_width, rows), BF16),
            pltpu.VMEM((2, half_width, rows), BF16),
            pltpu.VMEM((2, half_width, rows), F32),
            pltpu.VMEM((half_width, rows), F32),
            pltpu.VMEM((TICKS - 1, rows, width), BF16),
            dma((2,)),
            dma((2,)),
            dma((TICKS - 1,)),
            dma((TICKS - 1, half)),
            dma((TICKS - 1,)),
            dma((TICKS - 1,)),
            dma((TICKS,)),
            dma((TICKS,)),
            dma((TICKS,)),
            dma((TICKS,)),
            dma((TICKS - 1,)),
            dma((TICKS - 1,)),
            dma((2,)),
            dma((2,)),
            dma((2,)),
        ],
        compiler_params=pltpu.CompilerParams(
            collective_id=0, has_side_effects=True, vmem_limit_bytes=62 * 2**20 + 2**18
        ),
    )(
        inflow[0].reshape(2, rows, width),
        fresh_rows[:, 0],
        lin_weight[0].T,
        qkv_weight[0].transpose(0, 2, 1).reshape(3 * head_cols, width),
        out_weight[0],
        mod_weight[0].transpose(1, 2, 0).reshape(2 * half_width, FREQ),
        plan.T,
        timesteps.T,
    )
    return settled.T[None]


def solution(mesh):
    return jax.shard_map(
        on_device,
        mesh=mesh,
        in_specs=(
            P("section", ("groups", "replica"), None),
            P(None, ("groups", "replica"), "section", None),
            P("section", None, "tensor"),
            P("section", None, None, "tensor"),
            P("section", "tensor", None),
            P("section", None, None, "tensor"),
            P(None, "section"),
            P(None, ("groups", "replica")),
        ),
        out_specs=P("section", ("groups", "replica"), "tensor"),
        check_vma=False,
    )
```
